32 devices in a mesh: dp: 16 (over z, y, core), seq: 2 (over x).
Axes of the slice: x: 2, y: 2, z: 4, core: 2. Of those that a mesh axis runs over, the one named last changes fastest.
Arguments:
- latents: bfloat16 [16, 1024, 1152], P('dp', 'seq'), may hold values from -6 to 6
- condition: bfloat16 [16, 1152], P('dp'), may hold values from -6 to 6
- cotangent: bfloat16 [16, 1024, 1152], P('dp', 'seq'), may hold values from -6 to 6
- ada_w: bfloat16 [7962624], P(('dp', 'seq')), may hold values from -0.1875 to 0.1875
- qkv_w: bfloat16 [3981312], P(('dp', 'seq')), may hold values from -0.1875 to 0.1875
- proj_w: bfloat16 [1327104], P(('dp', 'seq')), may hold values from -1.5 to 1.5
- fc1_w: bfloat16 [5308416], P(('dp', 'seq')), may hold values from -0.1875 to 0.1875
- fc2_w: bfloat16 [5308416], P(('dp', 'seq')), may hold values from -0.09375 to 0.09375
- biases: bfloat16 [16128], P(('dp', 'seq')), may hold values from -3 to 3
Outputs:
- output: bfloat16 [16, 1024, 1152], P('dp', 'seq')
- grad_latents: float32 [16, 1024, 1152], P('dp', 'seq')
- grad_condition: float32 [16, 1152], P('dp')
- grad_ada: float32 [7962624], P(('dp', 'seq'))
- grad_qkv: float32 [3981312], P(('dp', 'seq'))
- grad_proj: float32 [1327104], P(('dp', 'seq'))
- grad_fc1: float32 [5308416], P(('dp', 'seq'))
- grad_fc2: float32 [5308416], P(('dp', 'seq'))
- grad_biases: float32 [16128], P(('dp', 'seq'))
The draws below stay inside these ranges and needn't reach their ends.
All inputs are finite; a program needn't handle non-finite values.
Results may differ from the reference program's by a relative error of at most 0.018.
The reference program's roundings to bfloat16 on the way count: a program that leaves them out, or rounds other values in their place, can miss the bound.
Values may be sent and summed in bfloat16 or wider, within the bound.
A program may use at most 384 MiB of HBM per device.

```python
import jax
import jax.numpy as jnp
from jax import lax

D = 1152
HEADS = 16
HD = 72
FF = 4608
LEN = 1024
LATENTS = 16
N_DP = 16
N_SEQ = 2


def level_of(own_key, shape, pieces, least, top_value):
    gain, own = 1.0, jax.random.fold_in(own_key, 6)
    for dim, shards_of in pieces:
        steps = jnp.exp(jax.random.uniform(jax.random.fold_in(own, dim), (shards_of,), jnp.float32, least / len(pieces), top_value / len(pieces)))
        gain = gain * jnp.repeat(steps, shape[dim] // shards_of).reshape([-1 if axis == dim else 1 for axis in range(len(shape))])
    return gain


def noise(key, extent, spread, limit, pieces=(), held_as=jnp.bfloat16):
    array = spread * jax.random.normal(key, extent, jnp.float32)
    if pieces:
        array = array * level_of(key, extent, pieces, -0.22, 0.18)
    return jnp.clip(array, -limit, limit).astype(held_as)


def setup_inputs(seed: int = 0) -> dict:
    streams_of = jax.random.split(jax.random.key(seed), 10)
    latents = noise(streams_of[0], (LATENTS, LEN, D), 1.0, 6.0, ((0, 16), (1, 2)))
    condition = noise(streams_of[1], (LATENTS, D), 1.0, 6.0, ((0, 16),))
    cotangent = noise(streams_of[2], (LATENTS, LEN, D), 1.0, 6.0, ((0, 16), (1, 2)))
    ada_w = noise(streams_of[3], (6 * D * D,), D ** -0.5, 0.1875, ((0, 32),))
    qkv_w = noise(streams_of[4], (3 * D * D,), D ** -0.5, 0.1875, ((0, 32),))
    proj_w = noise(streams_of[5], (D * D,), (D // 64) ** -0.5, 1.5, ((0, 32),))
    fc1_w = noise(streams_of[6], (D * FF,), D ** -0.5, 0.1875, ((0, 32),))
    fc2_w = noise(streams_of[7], (FF * D,), FF ** -0.5, 0.09375, ((0, 32),))
    biases = noise(streams_of[8], (10 * D + FF,), 0.5, 3.0, ((0, 32),))
    return {"latents": latents, "condition": condition, "cotangent": cotangent, "ada_w": ada_w, "qkv_w": qkv_w, "proj_w": proj_w, "fc1_w": fc1_w, "fc2_w": fc2_w, "biases": biases}


@jax.custom_vjp
def low(v):
    return lax.optimization_barrier(v.astype(jnp.bfloat16)).astype(jnp.float32)

@jax.custom_vjp
def low_back(v):
    return v

def low_keep(v):
    return (low(v), None)

def low_pass(kept, grad):
    return (grad,)

def back_keep(v):
    return (v, None)

def back_low(kept, grad):
    return (low(grad),)
low.defvjp(low_keep, low_pass)
low_back.defvjp(back_keep, back_low)

def matmul(left, right):
    return jnp.dot(left, right, precision=lax.Precision.HIGHEST)

def blocked(flat, height, breadth):
    return flat.reshape(N_DP, N_SEQ, height // N_DP, breadth // N_SEQ).transpose(0, 2, 1, 3).reshape(height, breadth)

def unblocked(matrix):
    height, breadth = matrix.shape
    return matrix.reshape(N_DP, height // N_DP, N_SEQ, breadth // N_SEQ).transpose(0, 2, 1, 3).reshape(-1)

def layer_norm(values):
    centred = values - lax.optimization_barrier(jnp.mean(values, axis=-1, keepdims=True))
    return centred * lax.rsqrt(lax.optimization_barrier(jnp.mean(centred * centred, axis=-1, keepdims=True)) + 1e-06)

def latent_forward(params, tokens, cond):
    w_ada, w_qkv, w_proj, w_up, w_down, b_all = params
    b_ada = b_all[:6 * D]
    b_qv = b_all[6 * D:8 * D]
    b_proj = b_all[8 * D:9 * D]
    b_up = b_all[9 * D:9 * D + FF]
    b_down = b_all[9 * D + FF:]
    act = low(jax.nn.silu(cond))
    modul = low_back(matmul(act[None, :], w_ada)[0] + b_ada)
    shift1 = modul[0:D]
    scale1 = modul[D:2 * D]
    gate1 = modul[2 * D:3 * D]
    shift2 = modul[3 * D:4 * D]
    scale2 = modul[4 * D:5 * D]
    gate2 = modul[5 * D:6 * D]
    first = low(layer_norm(tokens) * (1.0 + scale1) + shift1)
    qkv = matmul(first, w_qkv)
    query = low_back(low(qkv[:, :D] + b_qv[:D])).reshape(-1, HEADS, HD)
    keys = low_back(low(qkv[:, D:2 * D])).reshape(-1, HEADS, HD)
    values = low_back(low(qkv[:, 2 * D:] + b_qv[D:])).reshape(-1, HEADS, HD)
    scores = low_back(jnp.einsum('qhd,khd->hqk', query, keys, precision=lax.Precision.HIGHEST) * HD ** (-0.5))
    probs = low(jax.nn.softmax(scores, axis=-1))
    mixed = jnp.einsum('hqk,khd->qhd', probs, values, precision=lax.Precision.HIGHEST).reshape(-1, D)
    mixed = low_back(low(mixed))
    attn = low_back(matmul(mixed, w_proj) + b_proj)
    middle = tokens + gate1 * attn
    second = low(layer_norm(middle) * (1.0 + scale2) + shift2)
    upper = low_back(matmul(second, w_up) + b_up)
    hidden = low(jax.nn.gelu(upper, approximate=True))
    branch = low_back(matmul(hidden, w_down) + b_down)
    return middle + gate2 * branch

def reference(latents, condition, cotangent, ada_w, qkv_w, proj_w, fc1_w, fc2_w, biases):
    params = (blocked(ada_w.astype(jnp.float32), D, 6 * D), blocked(qkv_w.astype(jnp.float32), D, 3 * D), blocked(proj_w.astype(jnp.float32), D, D), blocked(fc1_w.astype(jnp.float32), D, FF), blocked(fc2_w.astype(jnp.float32), FF, D), biases.astype(jnp.float32))
    tokens = latents.astype(jnp.float32)
    cond = condition.astype(jnp.float32)
    stepper = jax.checkpoint(latent_forward)

    def whole(params, tokens, cond):

        def scan_step(carry, pair):
            return (carry, stepper(params, pair[0], pair[1]))
        carry, outs = lax.scan(scan_step, jnp.zeros((), jnp.float32), (tokens, cond))
        return outs
    output, pullback = jax.vjp(whole, params, tokens, cond)
    grad_params, grad_tokens, grad_cond = pullback(cotangent.astype(jnp.float32))
    return (output.astype(jnp.bfloat16), grad_tokens, grad_cond, unblocked(grad_params[0]), unblocked(grad_params[1]), unblocked(grad_params[2]), unblocked(grad_params[3]), unblocked(grad_params[4]), grad_params[5])
```

```python
import jax
import jax.numpy as jnp
from jax import lax
from jax.sharding import PartitionSpec as P

D = 1152
HEADS = 16
HD = 72
FF = 4608


def layer_norm(values):
    centred = values - jnp.mean(values, axis=-1, keepdims=True)
    return centred * lax.rsqrt(jnp.mean(centred * centred, axis=-1, keepdims=True) + 1e-06)


def gelu_tanh(values):
    return jax.nn.gelu(values, approximate=True)


def cross(left, right):
    return lax.dot_general(
        left, right, (((0,), (0,)), ((), ())), preferred_element_type=jnp.float32
    )


def against(left, right):
    return lax.dot_general(
        left, right, (((1,), (1,)), ((), ())), preferred_element_type=jnp.float32
    )


def swap(values, axis, stride):
    size = lax.axis_size(axis)
    return lax.ppermute(values, axis, [(d, d ^ stride) for d in range(size)])


def strides_of(size):
    return [1 << b for b in range(size.bit_length() - 1)]


def small_gather(values, axis):
    me = lax.axis_index(axis)
    for stride in strides_of(lax.axis_size(axis)):
        other = swap(values, axis, stride)
        low = (me & stride) == 0
        values = jnp.where(
            low,
            jnp.concatenate([values, other], axis=0),
            jnp.concatenate([other, values], axis=0),
        )
    return values


def halve_rows(values, axis_of, stride, wire):
    bit = (lax.axis_index("dp") // stride) % 2
    axis = axis_of.index(stride)
    send = lax.dynamic_index_in_dim(values, 1 - bit, axis, keepdims=False)
    keep = lax.dynamic_index_in_dim(values, bit, axis, keepdims=False)
    got = swap(send.astype(wire), "dp", stride)
    return (keep.astype(jnp.float32) + got.astype(jnp.float32)).astype(wire)


def reduce_scatter(columns, order, wire):
    n_rows = lax.axis_size("dp")
    axis_of = strides_of(n_rows)[::-1]
    height, width = columns[0].shape
    shape = (2,) * len(axis_of) + (height // n_rows, width)
    state = [c.reshape(shape) for c in columns]
    me_col = lax.axis_index("seq")
    for axis, stride in order:
        if axis == "dp":
            state = [halve_rows(s, axis_of, stride, wire) for s in state]
            axis_of = [s for s in axis_of if s != stride]
        else:
            half = len(state) // 2
            high = ((me_col // half) % 2) == 1
            nxt = []
            for a, b in zip(state[:half], state[half:]):
                send = jnp.where(high, a, b)
                keep = jnp.where(high, b, a)
                got = swap(send.astype(wire), "seq", half)
                nxt.append((keep.astype(jnp.float32) + got.astype(jnp.float32)).astype(wire))
            state = nxt
    return state[0]


def orders():
    rows = [("dp", s) for s in strides_of(lax.axis_size("dp"))]
    cols = [("seq", s) for s in strides_of(lax.axis_size("seq"))[::-1]]
    high = rows[2:][::-1]
    first = rows[:1] + cols + rows[1:2] + high
    second = rows[:1] + rows[1:2] + cols + high
    third = rows[:1] + high + rows[1:2] + cols
    return first, second, third


def shifted(values, shift):
    size = lax.axis_size("seq")
    return lax.ppermute(values, "seq", [(d, (d + shift) % size) for d in range(size)])


def to_heads(values):
    size = lax.axis_size("seq")
    me = lax.axis_index("seq")
    wide = D // size
    parts = values.shape[-1] // D

    def group(g):
        return jnp.concatenate(
            [lax.dynamic_slice_in_dim(values, p * D + g * wide, wide, 2) for p in range(parts)],
            axis=2,
        )

    got = [group(me)]
    for s in range(1, size):
        got.append(shifted(group((me + s) % size), s))
    whole = jnp.concatenate(got, axis=1)
    return [whole[:, :, p * wide : (p + 1) * wide] for p in range(parts)]


def to_tokens(pieces):
    size = lax.axis_size("seq")
    me = lax.axis_index("seq")
    wide = D // size
    parts = len(pieces)
    rows = pieces[0].shape[1] // size
    whole = jnp.concatenate(pieces, axis=2)
    got = [whole[:, :rows]]
    for s in range(1, size):
        got.append(shifted(whole[:, s * rows : (s + 1) * rows], -s))
    out = []
    for p in range(parts):
        mine = [g[:, :, p * wide : (p + 1) * wide] for g in got]
        if size == 2:
            out.append(
                jnp.where(
                    me == 0,
                    jnp.concatenate(mine, axis=2),
                    jnp.concatenate(mine[::-1], axis=2),
                )
            )
        else:
            full = jnp.zeros(whole.shape[:1] + (rows, D), whole.dtype)
            for s in range(size):
                full = lax.dynamic_update_slice_in_dim(
                    full, mine[s], ((me + s) % size) * wide, 2
                )
            out.append(full)
    return jnp.concatenate(out, axis=2)


def attend(query, keys, vals):
    lats, total, wide = query.shape
    heads = wide // HD
    q, k, v = [a.reshape(lats, total, heads, HD) for a in (query, keys, vals)]
    scores = jnp.einsum("bqhd,bkhd->bhqk", q, k, preferred_element_type=jnp.float32) * HD ** (-0.5)
    peak = jnp.max(scores, axis=-1, keepdims=True)
    expo = jnp.exp(scores - peak)
    summed = jnp.sum(expo, axis=-1, keepdims=True)
    logsum = peak + jnp.log(summed)
    probs = (expo / summed).astype(jnp.bfloat16)
    mixed = jnp.einsum("bhqk,bkhd->bqhd", probs, v, preferred_element_type=jnp.float32)
    return mixed.astype(jnp.bfloat16).reshape(lats, total, wide), logsum


def attend_back(query, keys, vals, d_mixed, logsum):
    lats, total, wide = query.shape
    heads = wide // HD
    scale = HD ** (-0.5)
    q, k, v, d = [a.reshape(lats, total, heads, HD) for a in (query, keys, vals, d_mixed)]
    again = jnp.einsum("bqhd,bkhd->bhqk", q, k, preferred_element_type=jnp.float32) * scale
    probs = jnp.exp(again - logsum)
    d_probs = jnp.einsum("bqhd,bkhd->bhqk", d, v, preferred_element_type=jnp.float32)
    inner = jnp.sum(d_probs * probs, axis=-1, keepdims=True)
    d_scores = (probs * (d_probs - inner)).astype(jnp.bfloat16)
    dq = jnp.einsum("bhqk,bkhd->bqhd", d_scores, k, preferred_element_type=jnp.float32) * scale
    dk = jnp.einsum("bhqk,bqhd->bkhd", d_scores, q, preferred_element_type=jnp.float32) * scale
    dv = jnp.einsum(
        "bhqk,bqhd->bkhd", probs.astype(jnp.bfloat16), d, preferred_element_type=jnp.float32
    )
    return [a.astype(jnp.bfloat16).reshape(lats, total, wide) for a in (dq, dk, dv)]


def times(left, columns):
    return jnp.concatenate(
        [jnp.dot(left, c, preferred_element_type=jnp.float32) for c in columns], axis=1
    )


def times_back(left, columns):
    width = columns[0].shape[1]
    return sum(against(left[:, j * width : (j + 1) * width], c) for j, c in enumerate(columns))


def weight_partials(left, right, n_cols):
    width = right.shape[1] // n_cols
    return [
        cross(left, right[:, j * width : (j + 1) * width]).astype(jnp.bfloat16)
        for j in range(n_cols)
    ]


def gathered(flat, height, breadth):
    n_rows, n_cols = lax.axis_size("dp"), lax.axis_size("seq")
    block = flat.reshape(1, height // n_rows, breadth // n_cols)
    whole = lax.all_gather(block, ("dp", "seq"), axis=0, tiled=True)
    whole = whole.reshape(n_rows, n_cols, height // n_rows, breadth // n_cols)
    return [whole[:, j].reshape(height, breadth // n_cols) for j in range(n_cols)]


def body(latents, condition, cotangent, ada_w, qkv_w, proj_w, fc1_w, fc2_w, biases):
    lats, rows, width = latents.shape
    count = lats * rows
    n_rows = lax.axis_size("dp")
    n_cols = lax.axis_size("seq")
    me_row, me_col = lax.axis_index("dp"), lax.axis_index("seq")
    by_x, by_y, by_z = orders()

    share = biases.shape[0]
    payload = jnp.concatenate([biases, condition.reshape(-1)]).reshape(1, -1)
    payload = small_gather(small_gather(payload, "seq"), "dp")
    b_all = payload[:, :share].reshape(-1).astype(jnp.float32)
    conds = payload[:, share:].reshape(n_rows, n_cols, lats, D)[:, 0].reshape(n_rows * lats, D)
    w_qkv = gathered(qkv_w, D, 3 * D)
    w_proj = gathered(proj_w, D, D)
    w_up = gathered(fc1_w, D, FF)
    w_down = gathered(fc2_w, FF, D)
    b_ada = b_all[: 6 * D]
    b_qv = b_all[6 * D : 8 * D]
    b_proj = b_all[8 * D : 9 * D]
    b_up = b_all[9 * D : 9 * D + FF]
    b_down = b_all[9 * D + FF :]

    ada_h, ada_c = D // n_rows, 6 * D // n_cols
    ada_block = ada_w.reshape(ada_h, ada_c)
    acts = jax.nn.silu(conds.astype(jnp.float32)).astype(jnp.bfloat16)
    acts_rows = lax.dynamic_slice_in_dim(acts, me_row * ada_h, ada_h, 1)
    part = jnp.dot(acts_rows, ada_block, preferred_element_type=jnp.float32)
    dp_order = [("dp", s) for s in strides_of(n_rows)[::-1]]
    part = reduce_scatter([part], dp_order, jnp.float32)
    modul = small_gather(part[None], "seq").transpose(1, 0, 2).reshape(lats, 6 * D) + b_ada
    shift1, scale1, gate1, shift2, scale2, gate2 = [
        modul[:, None, j * D : (j + 1) * D] for j in range(6)
    ]

    tokens = latents.astype(jnp.float32)
    norm1 = layer_norm(tokens)
    first = (norm1 * (1.0 + scale1) + shift1).astype(jnp.bfloat16).reshape(count, D)
    b_qkv = jnp.concatenate([b_qv[:D], jnp.zeros((D,), jnp.float32), b_qv[D:]])
    qkv = (times(first, w_qkv) + b_qkv).astype(jnp.bfloat16).reshape(lats, rows, 3 * D)
    query, keys, vals = to_heads(qkv)
    mixed_h, logsum = attend(query, keys, vals)
    mixed = to_tokens([mixed_h]).reshape(count, D)
    attn = (times(mixed, w_proj) + b_proj).reshape(lats, rows, D)
    middle = tokens + gate1 * attn
    norm2 = layer_norm(middle)
    second = (norm2 * (1.0 + scale2) + shift2).astype(jnp.bfloat16).reshape(count, D)
    upper = times(second, w_up) + b_up
    hidden = gelu_tanh(upper).astype(jnp.bfloat16)
    branch = (times(hidden, w_down) + b_down).reshape(lats, rows, D)
    output = (middle + gate2 * branch).astype(jnp.bfloat16)

    grad_out = cotangent.astype(jnp.float32)
    d_gate2 = jnp.sum(grad_out * branch, axis=1)
    d_branch = (gate2 * grad_out).astype(jnp.bfloat16).reshape(count, D)
    gb_down = jnp.sum(d_branch.astype(jnp.float32), axis=0)
    grad_down = reduce_scatter(weight_partials(hidden, d_branch, n_cols), by_x, jnp.bfloat16)
    d_hidden = times_back(d_branch, w_down)
    gelu_back = jax.vjp(gelu_tanh, upper)[1]
    d_upper = gelu_back(d_hidden)[0].astype(jnp.bfloat16)
    gb_up = jnp.sum(d_upper.astype(jnp.float32), axis=0)
    grad_up = reduce_scatter(weight_partials(second, d_upper, n_cols), by_y, jnp.bfloat16)
    d_second = times_back(d_upper, w_up).reshape(lats, rows, D)
    d_shift2 = jnp.sum(d_second, axis=1)
    d_scale2 = jnp.sum(d_second * norm2, axis=1)
    norm_back2 = jax.vjp(layer_norm, middle)[1]
    d_middle = grad_out + norm_back2(d_second * (1.0 + scale2))[0]
    d_gate1 = jnp.sum(d_middle * attn, axis=1)
    d_attn = (gate1 * d_middle).astype(jnp.bfloat16).reshape(count, D)
    gb_proj = jnp.sum(d_attn.astype(jnp.float32), axis=0)
    d_mixed = times_back(d_attn, w_proj).astype(jnp.bfloat16).reshape(lats, rows, D)
    grad_proj = reduce_scatter(weight_partials(mixed, d_attn, n_cols), by_z, jnp.bfloat16)
    d_mixed_h = to_heads(d_mixed)[0]
    d_qkv = to_tokens(attend_back(query, keys, vals, d_mixed_h, logsum)).reshape(count, 3 * D)
    gb_qkv = jnp.sum(d_qkv.astype(jnp.float32), axis=0)
    gb_qv = jnp.concatenate([gb_qkv[:D], gb_qkv[2 * D :]])
    grad_qkv = reduce_scatter(weight_partials(first, d_qkv, n_cols), by_x, jnp.bfloat16)
    d_first = times_back(d_qkv, w_qkv).reshape(lats, rows, D)
    d_shift1 = jnp.sum(d_first, axis=1)
    d_scale1 = jnp.sum(d_first * norm1, axis=1)
    norm_back1 = jax.vjp(layer_norm, tokens)[1]
    grad_latents = d_middle + norm_back1(d_first * (1.0 + scale1))[0]

    d_modul = jnp.concatenate([d_shift1, d_scale1, d_gate1, d_shift2, d_scale2, d_gate2], axis=1)
    for stride in strides_of(n_cols):
        d_modul = d_modul + swap(d_modul, "seq", stride)
    d_modul = d_modul.astype(jnp.bfloat16)
    modul_cols = small_gather(
        lax.dynamic_slice_in_dim(d_modul, me_col * ada_c, ada_c, 1), "dp"
    )
    grad_ada = cross(acts_rows, modul_cols)
    d_acts = against(modul_cols, ada_block)
    for stride in strides_of(n_cols):
        d_acts = d_acts + swap(d_acts, "seq", stride)
    d_acts = small_gather(d_acts[None], "dp")
    d_act = lax.dynamic_slice_in_dim(d_acts, me_row * lats, lats, 1)
    d_act = d_act.transpose(1, 0, 2).reshape(lats, D)
    silu_back = jax.vjp(jax.nn.silu, condition.astype(jnp.float32))[1]
    grad_condition = silu_back(d_act)[0]

    owner = (me_col == 0).astype(jnp.float32)
    gb_ada = jnp.sum(d_modul.astype(jnp.float32), axis=0) * owner
    bias_all = jnp.concatenate([gb_ada, gb_qv, gb_proj, gb_up, gb_down])
    bias_all = bias_all.reshape(n_rows, n_cols, share)
    bias_sum = reduce_scatter([bias_all[:, j] for j in range(n_cols)], by_z, jnp.float32)
    return (
        output,
        grad_latents,
        grad_condition,
        grad_ada.reshape(-1),
        grad_qkv.astype(jnp.float32).reshape(-1),
        grad_proj.astype(jnp.float32).reshape(-1),
        grad_up.astype(jnp.float32).reshape(-1),
        grad_down.astype(jnp.float32).reshape(-1),
        bias_sum.reshape(-1),
    )


def solution(mesh):
    return jax.shard_map(
        body,
        mesh=mesh,
        in_specs=(
            P("dp", "seq", None),
            P("dp", None),
            P("dp", "seq", None),
            P(("dp", "seq")),
            P(("dp", "seq")),
            P(("dp", "seq")),
            P(("dp", "seq")),
            P(("dp", "seq")),
            P(("dp", "seq")),
        ),
        out_specs=(
            P("dp", "seq", None),
            P("dp", "seq", None),
            P("dp", None),
            P(("dp", "seq")),
            P(("dp", "seq")),
            P(("dp", "seq")),
            P(("dp", "seq")),
            P(("dp", "seq")),
            P(("dp", "seq")),
        ),
        check_vma=False,
    )
```

```python
import jax
import jax.numpy as jnp
from jax import lax
from jax.sharding import PartitionSpec as P

D = 1152
HEADS = 16
HD = 72
FF = 4608


def layer_norm(values):
    centred = values - jnp.mean(values, axis=-1, keepdims=True)
    return centred * lax.rsqrt(jnp.mean(centred * centred, axis=-1, keepdims=True) + 1e-06)


def gelu_tanh(values):
    return jax.nn.gelu(values, approximate=True)


def cross(left, right):
    return lax.dot_general(
        left, right, (((0,), (0,)), ((), ())), preferred_element_type=jnp.float32
    )


def against(left, right):
    return lax.dot_general(
        left, right, (((1,), (1,)), ((), ())), preferred_element_type=jnp.float32
    )


def swap(values, axis, stride):
    size = lax.axis_size(axis)
    return lax.ppermute(values, axis, [(d, d ^ stride) for d in range(size)])


def strides_of(size):
    return [1 << b for b in range(size.bit_length() - 1)]


def small_gather(values, axis):
    me = lax.axis_index(axis)
    for stride in strides_of(lax.axis_size(axis)):
        other = swap(values, axis, stride)
        low = (me & stride) == 0
        values = jnp.where(
            low,
            jnp.concatenate([values, other], axis=0),
            jnp.concatenate([other, values], axis=0),
        )
    return values


def halve_rows(values, axis_of, stride, wire):
    bit = (lax.axis_index("dp") // stride) % 2
    axis = axis_of.index(stride)
    send = lax.dynamic_index_in_dim(values, 1 - bit, axis, keepdims=False)
    keep = lax.dynamic_index_in_dim(values, bit, axis, keepdims=False)
    got = swap(send.astype(wire), "dp", stride)
    return (keep.astype(jnp.float32) + got.astype(jnp.float32)).astype(wire)


class Scatter:
    def __init__(self, columns, order, wire):
        n_rows = lax.axis_size("dp")
        self.axis_of = strides_of(n_rows)[::-1]
        height, width = columns[0].shape
        shape = (2,) * len(self.axis_of) + (height // n_rows, width)
        self.state = [c.reshape(shape) for c in columns]
        self.order = list(order)
        self.wire = wire

    def step(self):
        if not self.order:
            return self
        axis, stride = self.order.pop(0)
        if axis == "dp":
            self.state = [halve_rows(s, self.axis_of, stride, self.wire) for s in self.state]
            self.axis_of = [s for s in self.axis_of if s != stride]
            return self
        half = len(self.state) // 2
        high = ((lax.axis_index("seq") // half) % 2) == 1
        nxt = []
        for a, b in zip(self.state[:half], self.state[half:]):
            send = jnp.where(high, a, b)
            keep = jnp.where(high, b, a)
            got = swap(send.astype(self.wire), "seq", half)
            total = keep.astype(jnp.float32) + got.astype(jnp.float32)
            nxt.append(total.astype(self.wire))
        self.state = nxt
        return self

    def result(self):
        while self.order:
            self.step()
        return self.state[0]


def reduce_scatter(columns, order, wire):
    return Scatter(columns, order, wire).result()


def tie(value, *scatters):
    held = [s.state for s in scatters]
    value, held = lax.optimization_barrier((value, held))
    for s, state in zip(scatters, held):
        s.state = state
    return value


def orders():
    rows = [("dp", s) for s in strides_of(lax.axis_size("dp"))]
    cols = [("seq", s) for s in strides_of(lax.axis_size("seq"))[::-1]]
    high = rows[2:][::-1]
    first = rows[:1] + cols + rows[1:2] + high
    second = rows[:1] + rows[1:2] + cols + high
    third = rows[:1] + high + rows[1:2] + cols
    return first, second, third


def shifted(values, shift):
    size = lax.axis_size("seq")
    return lax.ppermute(values, "seq", [(d, (d + shift) % size) for d in range(size)])


def to_heads(values):
    size = lax.axis_size("seq")
    me = lax.axis_index("seq")
    wide = D // size
    parts = values.shape[-1] // D

    def group(g):
        return jnp.concatenate(
            [lax.dynamic_slice_in_dim(values, p * D + g * wide, wide, 2) for p in range(parts)],
            axis=2,
        )

    got = [group(me)]
    for s in range(1, size):
        got.append(shifted(group((me + s) % size), s))
    whole = jnp.concatenate(got, axis=1)
    return [whole[:, :, p * wide : (p + 1) * wide] for p in range(parts)]


def to_tokens(pieces):
    size = lax.axis_size("seq")
    me = lax.axis_index("seq")
    wide = D // size
    parts = len(pieces)
    rows = pieces[0].shape[1] // size
    whole = jnp.concatenate(pieces, axis=2)
    got = [whole[:, :rows]]
    for s in range(1, size):
        got.append(shifted(whole[:, s * rows : (s + 1) * rows], -s))
    out = []
    for p in range(parts):
        mine = [g[:, :, p * wide : (p + 1) * wide] for g in got]
        if size == 2:
            out.append(
                jnp.where(
                    me == 0,
                    jnp.concatenate(mine, axis=2),
                    jnp.concatenate(mine[::-1], axis=2),
                )
            )
        else:
            full = jnp.zeros(whole.shape[:1] + (rows, D), whole.dtype)
            for s in range(size):
                full = lax.dynamic_update_slice_in_dim(
                    full, mine[s], ((me + s) % size) * wide, 2
                )
            out.append(full)
    return jnp.concatenate(out, axis=2)


def attend(query, keys, vals):
    lats, total, wide = query.shape
    heads = wide // HD
    q, k, v = [a.reshape(lats, total, heads, HD) for a in (query, keys, vals)]
    scores = jnp.einsum("bqhd,bkhd->bhqk", q, k, preferred_element_type=jnp.float32) * HD ** (-0.5)
    peak = jnp.max(scores, axis=-1, keepdims=True)
    expo = jnp.exp(scores - peak)
    summed = jnp.sum(expo, axis=-1, keepdims=True)
    logsum = peak + jnp.log(summed)
    probs = (expo / summed).astype(jnp.bfloat16)
    mixed = jnp.einsum("bhqk,bkhd->bqhd", probs, v, preferred_element_type=jnp.float32)
    return mixed.astype(jnp.bfloat16).reshape(lats, total, wide), logsum


def attend_back(query, keys, vals, d_mixed, logsum, down, up, proj):
    lats, total, wide = query.shape
    heads = wide // HD
    scale = HD ** (-0.5)
    q, k, v, d = [a.reshape(lats, total, heads, HD) for a in (query, keys, vals, d_mixed)]
    again = jnp.einsum("bqhd,bkhd->bhqk", q, k, preferred_element_type=jnp.float32) * scale
    probs = jnp.exp(again - logsum)
    d_probs = jnp.einsum("bqhd,bkhd->bhqk", d, v, preferred_element_type=jnp.float32)
    inner = jnp.sum(d_probs * probs, axis=-1, keepdims=True)
    inner = tie(inner, proj.step())
    d_scores = (probs * (d_probs - inner)).astype(jnp.bfloat16)
    d_scores = tie(d_scores, down.step())
    dv = jnp.einsum(
        "bhqk,bqhd->bkhd", probs.astype(jnp.bfloat16), d, preferred_element_type=jnp.float32
    )
    dv, d_scores = tie((dv, d_scores), up.step(), proj.step())
    dk = jnp.einsum("bhqk,bqhd->bkhd", d_scores, q, preferred_element_type=jnp.float32) * scale
    dk, d_scores = tie((dk, d_scores), down.step(), proj.step())
    dq = jnp.einsum("bhqk,bkhd->bqhd", d_scores, k, preferred_element_type=jnp.float32) * scale
    return [a.astype(jnp.bfloat16).reshape(lats, total, wide) for a in (dq, dk, dv)]


def times(left, columns):
    return jnp.concatenate(
        [jnp.dot(left, c, preferred_element_type=jnp.float32) for c in columns], axis=1
    )


def times_back(left, columns):
    width = columns[0].shape[1]
    return sum(against(left[:, j * width : (j + 1) * width], c) for j, c in enumerate(columns))


def weight_partials(left, right, n_cols):
    width = right.shape[1] // n_cols
    return [
        cross(left, right[:, j * width : (j + 1) * width]).astype(jnp.bfloat16)
        for j in range(n_cols)
    ]


def gathered(flat):
    n_rows, n_cols = lax.axis_size("dp"), lax.axis_size("seq")
    whole = lax.all_gather(flat[None], ("dp", "seq"), axis=0, tiled=True)
    return whole.reshape((n_rows, n_cols) + flat.shape)


def body(latents, condition, cotangent, ada_w, qkv_w, proj_w, fc1_w, fc2_w, biases):
    lats, rows, width = latents.shape
    count = lats * rows
    n_rows = lax.axis_size("dp")
    n_cols = lax.axis_size("seq")
    me_row, me_col = lax.axis_index("dp"), lax.axis_index("seq")
    by_x, by_y, by_z = orders()

    share = biases.shape[0]
    payload = jnp.concatenate([biases, condition.reshape(-1)]).reshape(1, -1)
    payload = small_gather(small_gather(payload, "seq"), "dp")
    b_all = payload[:, :share].reshape(-1).astype(jnp.float32)
    conds = payload[:, share:].reshape(n_rows, n_cols, lats, D)[:, 0].reshape(n_rows * lats, D)
    side, narrow, slabs = D // n_rows, D // n_cols, FF // D
    whole = gathered(
        jnp.concatenate([qkv_w.reshape(side, 3 * narrow), proj_w.reshape(side, narrow)], axis=1)
    )
    w_qkv = [whole[:, j, :, : 3 * narrow].reshape(D, 3 * narrow) for j in range(n_cols)]
    w_proj = [whole[:, j, :, 3 * narrow :].reshape(D, narrow) for j in range(n_cols)]
    fc2_wide = fc2_w.reshape(slabs, side, narrow)
    fc2_wide = jnp.concatenate([fc2_wide[p] for p in range(slabs)], axis=1)
    whole = gathered(jnp.stack([fc1_w.reshape(side, slabs * narrow), fc2_wide]))
    w_up = [whole[:, j, 0].reshape(D, slabs * narrow) for j in range(n_cols)]
    w_down = [
        jnp.stack(
            [whole[:, j, 1, :, p * narrow : (p + 1) * narrow] for p in range(slabs)], axis=1
        ).reshape(FF, narrow)
        for j in range(n_cols)
    ]
    b_ada = b_all[: 6 * D]
    b_qv = b_all[6 * D : 8 * D]
    b_proj = b_all[8 * D : 9 * D]
    b_up = b_all[9 * D : 9 * D + FF]
    b_down = b_all[9 * D + FF :]

    ada_h, ada_c = D // n_rows, 6 * D // n_cols
    ada_block = ada_w.reshape(ada_h, ada_c)
    acts = jax.nn.silu(conds.astype(jnp.float32)).astype(jnp.bfloat16)
    acts_rows = lax.dynamic_slice_in_dim(acts, me_row * ada_h, ada_h, 1)
    part = jnp.dot(acts_rows, ada_block, preferred_element_type=jnp.float32)
    dp_order = [("dp", s) for s in strides_of(n_rows)[::-1]]
    part = reduce_scatter([part], dp_order, jnp.float32)
    modul = small_gather(part[None], "seq").transpose(1, 0, 2).reshape(lats, 6 * D) + b_ada
    shift1, scale1, gate1, shift2, scale2, gate2 = [
        modul[:, None, j * D : (j + 1) * D] for j in range(6)
    ]

    tokens = latents.astype(jnp.float32)
    norm1 = layer_norm(tokens)
    first = (norm1 * (1.0 + scale1) + shift1).astype(jnp.bfloat16).reshape(count, D)
    b_qkv = jnp.concatenate([b_qv[:D], jnp.zeros((D,), jnp.float32), b_qv[D:]])
    qkv = (times(first, w_qkv) + b_qkv).astype(jnp.bfloat16).reshape(lats, rows, 3 * D)
    query, keys, vals = to_heads(qkv)
    mixed_h, logsum = attend(query, keys, vals)
    mixed = to_tokens([mixed_h]).reshape(count, D)
    attn = (times(mixed, w_proj) + b_proj).reshape(lats, rows, D)
    middle = tokens + gate1 * attn
    norm2 = layer_norm(middle)
    second = (norm2 * (1.0 + scale2) + shift2).astype(jnp.bfloat16).reshape(count, D)
    upper = times(second, w_up) + b_up
    hidden = gelu_tanh(upper).astype(jnp.bfloat16)
    branch = (times(hidden, w_down) + b_down).reshape(lats, rows, D)
    output = (middle + gate2 * branch).astype(jnp.bfloat16)

    grad_out = cotangent.astype(jnp.float32)
    d_gate2 = jnp.sum(grad_out * branch, axis=1)
    d_branch = (gate2 * grad_out).astype(jnp.bfloat16).reshape(count, D)
    gb_down = jnp.sum(d_branch.astype(jnp.float32), axis=0)
    down = Scatter(weight_partials(hidden, d_branch, n_cols), by_y, jnp.bfloat16)
    d_branch = tie(d_branch, down)
    d_hidden = times_back(d_branch, w_down)
    gelu_back = jax.vjp(gelu_tanh, upper)[1]
    d_upper = gelu_back(d_hidden)[0].astype(jnp.bfloat16)
    gb_up = jnp.sum(d_upper.astype(jnp.float32), axis=0)
    d_upper = tie(d_upper, down.step())
    up = Scatter(weight_partials(second, d_upper, n_cols), by_x, jnp.bfloat16)
    d_upper = tie(d_upper, up)
    d_second = times_back(d_upper, w_up).reshape(lats, rows, D)
    d_shift2 = jnp.sum(d_second, axis=1)
    d_scale2 = jnp.sum(d_second * norm2, axis=1)
    norm_back2 = jax.vjp(layer_norm, middle)[1]
    d_middle = grad_out + norm_back2(d_second * (1.0 + scale2))[0]
    d_gate1 = jnp.sum(d_middle * attn, axis=1)
    d_attn = (gate1 * d_middle).astype(jnp.bfloat16).reshape(count, D)
    gb_proj = jnp.sum(d_attn.astype(jnp.float32), axis=0)
    d_mixed = times_back(d_attn, w_proj).astype(jnp.bfloat16).reshape(lats, rows, D)
    proj = Scatter(weight_partials(mixed, d_attn, n_cols), by_z, jnp.bfloat16)
    d_mixed_h = tie(to_heads(d_mixed)[0], proj, up.step())
    d_heads = attend_back(query, keys, vals, d_mixed_h, logsum, down, up, proj)
    d_qkv = to_tokens(tie(d_heads, up.step(), proj.step())).reshape(count, 3 * D)
    d_qkv = tie(d_qkv, down.step(), up.step(), proj.step())
    gb_qkv = jnp.sum(d_qkv.astype(jnp.float32), axis=0)
    gb_qv = jnp.concatenate([gb_qkv[:D], gb_qkv[2 * D :]])
    partials = weight_partials(first, d_qkv, n_cols)
    cut = partials[0].shape[1] // 256 * 128
    left = Scatter([p[:, :cut] for p in partials], by_x, jnp.bfloat16)
    right = Scatter([p[:, cut:] for p in partials], by_y, jnp.bfloat16)
    d_qkv = tie(d_qkv, left, right)
    d_first = times_back(d_qkv, w_qkv).reshape(lats, rows, D)
    d_first = tie(d_first, left.step(), right.step(), down.step(), up.step())
    d_shift1 = jnp.sum(d_first, axis=1)
    d_scale1 = jnp.sum(d_first * norm1, axis=1)
    norm_back1 = jax.vjp(layer_norm, tokens)[1]
    grad_latents = d_middle + norm_back1(d_first * (1.0 + scale1))[0]

    d_modul = jnp.concatenate([d_shift1, d_scale1, d_gate1, d_shift2, d_scale2, d_gate2], axis=1)
    for stride in strides_of(n_cols):
        d_modul = d_modul + swap(d_modul, "seq", stride)
    d_modul = d_modul.astype(jnp.bfloat16)
    modul_cols = small_gather(
        lax.dynamic_slice_in_dim(d_modul, me_col * ada_c, ada_c, 1), "dp"
    )
    modul_cols = tie(modul_cols, left.step(), right.step())
    grad_ada = cross(acts_rows, modul_cols)
    d_acts = against(modul_cols, ada_block)
    for stride in strides_of(n_cols):
        d_acts = d_acts + swap(d_acts, "seq", stride)
    d_acts = small_gather(d_acts[None], "dp")
    d_acts = tie(d_acts, left.step(), right.step())
    grad_down, grad_up, grad_proj = down.result(), up.result(), proj.result()
    grad_qkv = jnp.concatenate([left.result(), right.result()], axis=1)
    d_act = lax.dynamic_slice_in_dim(d_acts, me_row * lats, lats, 1)
    d_act = d_act.transpose(1, 0, 2).reshape(lats, D)
    silu_back = jax.vjp(jax.nn.silu, condition.astype(jnp.float32))[1]
    grad_condition = silu_back(d_act)[0]

    owner = (me_col == 0).astype(jnp.float32)
    gb_ada = jnp.sum(d_modul.astype(jnp.float32), axis=0) * owner
    bias_all = jnp.concatenate([gb_ada, gb_qv, gb_proj, gb_up, gb_down])
    bias_order = [("seq", s) for s in strides_of(n_cols)[::-1]] + dp_order
    bias_all = bias_all.reshape(n_rows, n_cols, share)
    bias_sum = reduce_scatter([bias_all[:, j] for j in range(n_cols)], bias_order, jnp.float32)
    return (
        output,
        grad_latents,
        grad_condition,
        grad_ada.reshape(-1),
        grad_qkv.astype(jnp.float32).reshape(-1),
        grad_proj.astype(jnp.float32).reshape(-1),
        grad_up.astype(jnp.float32).reshape(-1),
        grad_down.astype(jnp.float32).reshape(-1),
        bias_sum.reshape(-1),
    )


def solution(mesh):
    return jax.shard_map(
        body,
        mesh=mesh,
        in_specs=(
            P("dp", "seq", None),
            P("dp", None),
            P("dp", "seq", None),
            P(("dp", "seq")),
            P(("dp", "seq")),
            P(("dp", "seq")),
            P(("dp", "seq")),
            P(("dp", "seq")),
            P(("dp", "seq")),
        ),
        out_specs=(
            P("dp", "seq", None),
            P("dp", "seq", None),
            P("dp", None),
            P(("dp", "seq")),
            P(("dp", "seq")),
            P(("dp", "seq")),
            P(("dp", "seq")),
            P(("dp", "seq")),
            P(("dp", "seq")),
        ),
        check_vma=False,
    )
```
